256 devices in a mesh: seq: 16 (over y, x), branch: 8 (over z), dp: 2 (over core).
Axes of the slice: x: 4, y: 4, z: 8, core: 2. Of those that a mesh axis runs over, the one named last changes fastest.
Arguments:
- query: bfloat16 [32768, 2048], P(('dp', 'seq', 'branch')), parts along dimension 0, may hold values from -4.5 to 4.5
- resp_key: bfloat16 [32768, 256], P(('dp', 'seq', 'branch')), parts along dimension 0, may hold values from -4.5 to 4.5
- resp_value: bfloat16 [32768, 256], P(('dp', 'seq', 'branch')), parts along dimension 0, may hold values from -4.5 to 4.5
- out_grad: bfloat16 [32768, 2048], P(('dp', 'seq', 'branch')), parts along dimension 0, may hold values from -4.5 to 4.5
- prompt_key: bfloat16 [2048, 256], P(('dp', 'seq')), parts along dimension 0, may hold values from -4.5 to 4.5
- prompt_value: bfloat16 [2048, 256], P(('dp', 'seq')), parts along dimension 0, may hold values from -4.5 to 4.5
- prefix_blocks: int32 [32], P(('dp', 'seq')), parts along dimension 0, may hold values from 1 to 16, as said below
Outputs:
- query_grad: bfloat16 [32768, 2048], P(('dp', 'seq', 'branch')), parts along dimension 0
- resp_key_grad: bfloat16 [32768, 256], P(('dp', 'seq', 'branch')), parts along dimension 0
- resp_value_grad: bfloat16 [32768, 256], P(('dp', 'seq', 'branch')), parts along dimension 0
- prompt_key_grad: bfloat16 [2048, 256], P(('dp', 'seq')), parts along dimension 0
- prompt_value_grad: bfloat16 [2048, 256], P(('dp', 'seq')), parts along dimension 0
The draws below stay inside these ranges and needn't reach their ends.
There are 2 independent parts, one for each index of `dp`. The reference program is written for one: setup_inputs(seed, part) draws one part's arguments, and reference() takes and returns one part's arrays. A program takes and returns all parts, laid end to end along the dimension named above; each array names one. Nothing has to cross between parts.
Inputs may be any that keep to these rules, and one draw needn't show every extreme that they name: `prefix_blocks`: some response sees the whole prompt and some response only its first 64 tokens.
All inputs are finite; a program needn't handle non-finite values.
Results may differ from the reference program's by a relative error of at most 0.017.
Values may be sent and summed in bfloat16 or wider, within the bound.
No kernel may reach another device: no remote copies, remote signals or barrier semaphores. Data moves between devices by JAX's collectives and lax.ppermute only.
A program may use at most 64 MiB of HBM per device.

```python
import math
import jax
import jax.numpy as jnp
from jax import lax

HD = 128
HQ = 8
G = 2
PDEV = 64
RESPONSES = 16
RLEN = 1024
PROMPT = 1024
ROWS = 16384


def draw_query(key, part):
    key = jax.random.fold_in(key, 5)
    base = jnp.clip(jax.random.normal(key, (ROWS, G * HQ * HD), jnp.float32), -4.5, 4.5)
    return base.astype(jnp.bfloat16)


def draw_prompt_key(key, part):
    key = jax.random.fold_in(key, 3)
    base = jnp.clip(jax.random.normal(key, (PROMPT, G * HD), jnp.float32), -4.5, 4.5)
    return base.astype(jnp.bfloat16)


def draw_prefix_blocks(key, part):
    key = jax.random.fold_in(key, 11)
    entry_count = RESPONSES
    widest = PROMPT // PDEV
    values = jax.random.randint(key, (entry_count,), 1, widest + 1)
    top_spot = jax.random.randint(jax.random.fold_in(key, 1), (), 0, entry_count)
    low_spot = (top_spot + 1 + jax.random.randint(jax.random.fold_in(key, 2), (), 0, entry_count - 1)) % entry_count
    entries = jnp.arange(entry_count)
    values = jnp.where(entries == top_spot, widest, values)
    values = jnp.where(entries == low_spot, 1, values)
    return values.astype(jnp.int32)


def level_of(rng, shape, shards, smallest, high):
    factor_of, own = 1.0, jax.random.fold_in(rng, 6)
    for dim, parts in shards:
        heights = jnp.exp(jax.random.uniform(jax.random.fold_in(own, dim), (parts,), jnp.float32, smallest / len(shards), high / len(shards)))
        factor_of = factor_of * jnp.repeat(heights, shape[dim] // parts).reshape([-1 if axis == dim else 1 for axis in range(len(shape))])
    return factor_of


def scatter_about(rng, dims, width, reach, split=(), held_as=jnp.bfloat16):
    level = level_of(rng, dims, split, -0.22, 0.18) if split else 1.0
    drawn = jax.random.normal(rng, dims, jnp.float32) * width * level
    return jnp.minimum(jnp.maximum(drawn, -reach), reach).astype(held_as)


def setup_inputs(seed: int = 0, part: int = 0) -> dict:
    splits = jax.random.split(jax.random.key(seed), 8)
    own_keys = jax.random.split(jax.random.fold_in(splits[7], part), 8)
    return {
        "query": draw_query(jax.random.fold_in(jax.random.fold_in(splits[7], part), 71), part),
        "resp_key": scatter_about(own_keys[1], (ROWS, G * HD), 1.0, 4.5, ((0, 128),)),
        "resp_value": scatter_about(own_keys[2], (ROWS, G * HD), 1.0, 4.5, ((0, 128),)),
        "out_grad": scatter_about(own_keys[3], (ROWS, G * HQ * HD), 1.0, 4.5, ((0, 128),)),
        "prompt_key": draw_prompt_key(jax.random.fold_in(jax.random.fold_in(splits[7], part), 71), part),
        "prompt_value": scatter_about(own_keys[5], (PROMPT, G * HD), 1.0, 4.5, ((0, 16),)),
        "prefix_blocks": draw_prefix_blocks(jax.random.fold_in(jax.random.fold_in(splits[7], part), 71), part),
    }


def response_grads(query, resp_key, resp_value, out_grad, prompt_key, prompt_value, prefix):
    row_count = query.shape[0]
    scaling = 1.0 / math.sqrt(HD)
    visible = prefix * PDEV
    prompt_mask = jnp.broadcast_to(jnp.arange(PROMPT, dtype=jnp.int32)[None, :] < visible, (row_count, PROMPT))
    positions = jnp.arange(row_count, dtype=jnp.int32)
    local_mask = positions[None, :] <= positions[:, None]
    key_mask = jnp.concatenate([prompt_mask, local_mask], axis=1)
    queries = query.astype(jnp.float32).reshape(row_count, G, HQ, HD)
    grads_out = jnp.transpose(out_grad.astype(jnp.float32).reshape(row_count, G, HQ, HD), (1, 2, 0, 3))
    all_keys = jnp.concatenate([prompt_key, resp_key], axis=0).astype(jnp.float32).reshape(-1, G, HD)
    all_values = jnp.concatenate([prompt_value, resp_value], axis=0).astype(jnp.float32).reshape(-1, G, HD)
    scores = jnp.einsum('rghd,kgd->ghrk', queries, all_keys) * scaling
    scores = jnp.where(key_mask[None, None], scores, -jnp.inf)
    row_max = lax.optimization_barrier(jnp.max(scores, axis=-1, keepdims=True))
    expo = jnp.exp(scores - row_max)
    probs = expo / lax.optimization_barrier(jnp.sum(expo, axis=-1, keepdims=True))
    probs_low = lax.optimization_barrier(probs.astype(jnp.bfloat16)).astype(jnp.float32)
    attn_out = jnp.einsum('ghrk,kgd->ghrd', probs_low, all_values)
    row_delta = lax.optimization_barrier(jnp.sum(grads_out * attn_out, axis=-1))
    prob_grad = jnp.einsum('ghrd,kgd->ghrk', grads_out, all_values)
    score_grad = probs * (prob_grad - row_delta[..., None])
    score_low = lax.optimization_barrier(score_grad.astype(jnp.bfloat16)).astype(jnp.float32)
    query_grad = jnp.einsum('ghrk,kgd->rghd', score_low, all_keys) * scaling
    key_grad = jnp.einsum('ghrk,rghd->kgd', score_low, queries) * scaling
    value_grad = jnp.einsum('ghrk,ghrd->kgd', probs_low, grads_out)
    return (query_grad.reshape(row_count, G * HQ * HD), key_grad.reshape(-1, G * HD), value_grad.reshape(-1, G * HD))

def reference(query, resp_key, resp_value, out_grad, prompt_key, prompt_value, prefix_blocks):

    def split_rows(array):
        return array.reshape((RESPONSES, RLEN) + array.shape[1:])

    def visit_response(carried, pieces):
        query_grad, key_grad, value_grad = response_grads(pieces[0], pieces[1], pieces[2], pieces[3], prompt_key, prompt_value, pieces[4])
        carried = (carried[0] + key_grad[:PROMPT], carried[1] + value_grad[:PROMPT])
        return (carried, (query_grad.astype(jnp.bfloat16), key_grad[PROMPT:].astype(jnp.bfloat16), value_grad[PROMPT:].astype(jnp.bfloat16)))
    zeros = jnp.zeros((PROMPT, G * HD), jnp.float32)
    totals, outputs = lax.scan(visit_response, (zeros, zeros), (split_rows(query), split_rows(resp_key), split_rows(resp_value), split_rows(out_grad), prefix_blocks))
    return (outputs[0].reshape(ROWS, G * HQ * HD), outputs[1].reshape(ROWS, G * HD), outputs[2].reshape(ROWS, G * HD), totals[0].astype(jnp.bfloat16), totals[1].astype(jnp.bfloat16))
```

```python
import functools
import math

import jax
import jax.numpy as jnp
from jax import lax
from jax.experimental import pallas as pl
from jax.experimental.pallas import tpu as pltpu
from jax.sharding import PartitionSpec as P

HD = 128
HQ = 8
G = 2
KV = G * HD
SCALE = 1.0 / math.sqrt(HD)
LOG2_SCALE = SCALE * math.log2(math.e)
MASKED = -1e30
SIDE = 4
F32 = jnp.float32
BF16 = jnp.bfloat16


def fold(x, op):
    return op(x.reshape(x.shape[0] // 8, 8, x.shape[1]), axis=0)


def kernel(rows, prompt_len, resp_len, n_branch, refs):
    place_ref, query_ref, grad_ref = refs[:3]
    resp_in = refs[3 : 3 + n_branch]
    prompt_in = refs[3 + n_branch : 3 + n_branch + SIDE]
    outs = refs[3 + n_branch + SIDE :]
    dq_ref = outs[0]
    resp_out = outs[1 : 1 + n_branch]
    prompt_out = outs[1 + n_branch : 1 + n_branch + SIDE]
    kv_buf, out_buf, q_t, g_t, s_buf, e_buf, dp_buf, dq_t = outs[1 + n_branch + SIDE :]

    blocks, branch, at_y, at_x = place_ref[0], place_ref[1], place_ref[2], place_ref[3]
    shard = prompt_len // (SIDE * SIDE)
    width = HQ * rows

    def prompt_place(dy, dx):
        y = lax.rem(at_y - dy + SIDE, SIDE)
        x = lax.rem(at_x - dx + SIDE, SIDE)
        return pl.multiple_of((y * SIDE + x) * shard, shard)

    def resp_place(s):
        return pl.multiple_of(prompt_len + lax.rem(branch - s + n_branch, n_branch) * rows, rows)

    for s in range(n_branch):
        kv_buf[pl.ds(resp_place(s), rows), :] = resp_in[s][...]
    for dy in range(SIDE):
        for dx in range(SIDE):
            kv_buf[pl.ds(prompt_place(dy, dx), shard), :] = prompt_in[dy][dx * shard : (dx + 1) * shard, :]
    out_buf[...] = jnp.zeros_like(out_buf)
    for g in range(G):
        for h in range(HQ):
            col = (g * HQ + h) * HD
            q_t[g, :, h * rows : (h + 1) * rows] = query_ref[:, col : col + HD].T
            g_t[g, :, h * rows : (h + 1) * rows] = grad_ref[:, col : col + HD].T
    dq_t[...] = jnp.zeros_like(dq_t)

    prompt_wide = blocks // 4
    wide_count = prompt_wide + branch // 2
    prompt_rest = lax.rem(blocks, 4)
    rest_count = prompt_rest + 2 * lax.rem(branch, 2)

    def wide_place(t):
        return pl.multiple_of(
            jnp.where(t < prompt_wide, t * 256, prompt_len + (t - prompt_wide) * 256), 256
        )

    def rest_place(t):
        return pl.multiple_of(
            jnp.where(
                t < prompt_rest,
                prompt_wide * 256 + t * 64,
                prompt_len + (branch // 2) * 256 + (t - prompt_rest) * 64,
            ),
            64,
        )

    diag_place = pl.multiple_of(prompt_len + branch * rows, rows)

    def visit(body, held):
        held = lax.fori_loop(0, wide_count, lambda t, c: body(c, wide_place(t), 256, False), held)
        held = lax.fori_loop(0, rest_count, lambda t, c: body(c, rest_place(t), 64, False), held)
        return body(held, diag_place, rows, True)

    def scores(held, at, size, diag):
        maxes = []
        for g in range(G):
            keys = kv_buf[pl.ds(at, size), g * HD : (g + 1) * HD]
            s = jnp.dot(keys, q_t[g], preferred_element_type=F32)
            if diag:
                key_pos = lax.broadcasted_iota(jnp.int32, (size, rows), 0)
                row_pos = lax.broadcasted_iota(jnp.int32, (size, rows), 1)
                seen = jnp.concatenate([key_pos <= row_pos] * HQ, axis=1)
                s = jnp.where(seen, s, MASKED)
            s_buf[g, pl.ds(at, size), :] = s
            maxes.append(jnp.maximum(held[g], fold(s, jnp.max)))
        return tuple(maxes)

    tops = visit(scores, tuple(jnp.full((8, width), MASKED, F32) for _ in range(G)))
    tops = [jnp.max(t, axis=0, keepdims=True) * LOG2_SCALE for t in tops]

    def weigh(held, at, size, diag):
        sums = []
        for g in range(G):
            values = kv_buf[pl.ds(at, size), KV + g * HD : KV + (g + 1) * HD]
            dp = jnp.dot(values, g_t[g], preferred_element_type=F32)
            e = jnp.exp2(s_buf[g, pl.ds(at, size), :] * LOG2_SCALE - tops[g])
            e_buf[g, pl.ds(at, size), :] = e.astype(BF16)
            dp_buf[g, pl.ds(at, size), :] = dp.astype(BF16)
            sums.append(held[2 * g] + fold(e, jnp.sum))
            sums.append(held[2 * g + 1] + fold(e * dp, jnp.sum))
        return tuple(sums)

    sums = visit(weigh, tuple(jnp.zeros((8, width), F32) for _ in range(2 * G)))
    weights, deltas = [], []
    for g in range(G):
        w = 1.0 / jnp.sum(sums[2 * g], axis=0, keepdims=True)
        weights.append(w)
        deltas.append(jnp.sum(sums[2 * g + 1], axis=0, keepdims=True) * w)
        q_t[g] = (q_t[g].astype(F32) * (w * SCALE)).astype(BF16)
        g_t[g] = (g_t[g].astype(F32) * w).astype(BF16)

    def grads(held, at, size, diag):
        for g in range(G):
            e = e_buf[g, pl.ds(at, size), :]
            ds = (e.astype(F32) * (dp_buf[g, pl.ds(at, size), :].astype(F32) - deltas[g])).astype(BF16)
            keys = kv_buf[pl.ds(at, size), g * HD : (g + 1) * HD]
            contract_rows = (((1,), (1,)), ((), ()))
            dk = lax.dot_general(ds, q_t[g], contract_rows, preferred_element_type=F32)
            dv = lax.dot_general(e, g_t[g], contract_rows, preferred_element_type=F32)
            out_buf[pl.ds(at, size), g * HD : (g + 1) * HD] = dk.astype(BF16)
            out_buf[pl.ds(at, size), KV + g * HD : KV + (g + 1) * HD] = dv.astype(BF16)
            dq_t[g] += jnp.dot(keys.T, ds, preferred_element_type=F32)
        return held

    visit(grads, 0)
    for g in range(G):
        dq = dq_t[g] * (weights[g] * SCALE)
        for h in range(HQ):
            col = (g * HQ + h) * HD
            dq_ref[:, col : col + HD] = dq[:, h * rows : (h + 1) * rows].T.astype(BF16)
    for s in range(n_branch):
        resp_out[s][...] = out_buf[pl.ds(resp_place(s), rows), :]
    for dy in range(SIDE):
        for dx in range(SIDE):
            prompt_out[dy][dx * shard : (dx + 1) * shard, :] = out_buf[pl.ds(prompt_place(dy, dx), shard), :]


def local_backward(place, query, out_grad, resp_blocks, prompt_blocks):
    rows = query.shape[0]
    n_branch = len(resp_blocks)
    resp_len = rows * n_branch
    prompt_len = SIDE * prompt_blocks[0].shape[0]
    keys, width = prompt_len + resp_len, HQ * rows
    vmem = pl.BlockSpec(memory_space=pltpu.VMEM)
    smem = pl.BlockSpec(memory_space=pltpu.SMEM)

    def body(*refs):
        kernel(rows, prompt_len, resp_len, n_branch, refs)

    return pl.pallas_call(
        body,
        out_shape=(
            [jax.ShapeDtypeStruct(query.shape, BF16)]
            + [jax.ShapeDtypeStruct((rows, 2 * KV), BF16)] * n_branch
            + [jax.ShapeDtypeStruct((prompt_len // SIDE, 2 * KV), BF16)] * SIDE
        ),
        in_specs=[smem] + [vmem] * (2 + n_branch + SIDE),
        out_specs=[vmem] * (1 + n_branch + SIDE),
        scratch_shapes=[
            pltpu.VMEM((keys, 2 * KV), BF16),
            pltpu.VMEM((keys, 2 * KV), BF16),
            pltpu.VMEM((G, HD, width), BF16),
            pltpu.VMEM((G, HD, width), BF16),
            pltpu.VMEM((G, keys, width), F32),
            pltpu.VMEM((G, keys, width), BF16),
            pltpu.VMEM((G, keys, width), BF16),
            pltpu.VMEM((G, HD, width), F32),
        ],
        compiler_params=pltpu.CompilerParams(vmem_limit_bytes=52 * 1024 * 1024),
        cost_estimate=pl.CostEstimate(flops=10 * G * width * keys * HD, bytes_accessed=4 << 20, transcendentals=G * width * keys),
    )(place, query, out_grad, *resp_blocks, *prompt_blocks)


def turn(n, step):
    return [(i, (i + step) % n) for i in range(n)]


def turn_seq(dy, dx):
    return [
        (y * SIDE + x, ((y + dy) % SIDE) * SIDE + (x + dx) % SIDE)
        for y in range(SIDE)
        for x in range(SIDE)
    ]


def add(x, y):
    return x.astype(F32) + y.astype(F32)


def on_device(query, resp_key, resp_value, out_grad, prompt_key, prompt_value, prefix_blocks, *, n_branch):
    shard = prompt_key.shape[0]
    half = n_branch // 2
    own_kv = jnp.concatenate([resp_key, resp_value], axis=1)
    own_prompt = jnp.concatenate([prompt_key, prompt_value], axis=1)

    resp_blocks = [own_kv] + [None] * (n_branch - 1)
    up = down = own_kv
    prompt_row = [own_prompt]
    prompt_blocks = None
    for step in range(1, half + 1):
        up = lax.ppermute(up, "branch", turn(n_branch, 1))
        resp_blocks[step] = up
        if step < half:
            down = lax.ppermute(down, "branch", turn(n_branch, -1))
            resp_blocks[n_branch - step] = down
    for dx in range(1, SIDE):
        prompt_row.append(lax.ppermute(own_prompt, "seq", turn_seq(0, dx)))
    prompt_row = jnp.concatenate(prompt_row, axis=0)
    prompt_blocks = [prompt_row] + [
        lax.ppermute(prompt_row, "seq", turn_seq(dy, 0)) for dy in range(1, SIDE)
    ]

    seq_at = lax.axis_index("seq")
    place = jnp.stack(
        [prefix_blocks[0], lax.axis_index("branch"), seq_at // SIDE, seq_at % SIDE]
    ).astype(jnp.int32)
    outs = local_backward(place, query, out_grad, resp_blocks, prompt_blocks)
    query_grad, resp_out, prompt_out = outs[0], outs[1 : 1 + n_branch], outs[1 + n_branch :]

    rows_y = prompt_out[0].astype(F32)
    for dy in range(1, SIDE):
        rows_y = add(rows_y, lax.ppermute(prompt_out[dy], "seq", turn_seq(-dy, 0)))
    rows_y = rows_y.astype(BF16)
    total = rows_y[:shard].astype(F32)
    for dx in range(1, SIDE):
        piece = rows_y[dx * shard : (dx + 1) * shard]
        total = add(total, lax.ppermute(piece, "seq", turn_seq(0, -dx)))

    down = resp_out[half]
    for s in range(half - 1, 0, -1):
        down = add(lax.ppermute(down, "branch", turn(n_branch, -1)), resp_out[s]).astype(BF16)
    down = lax.ppermute(down, "branch", turn(n_branch, -1))
    up = resp_out[half + 1]
    for s in range(half + 2, n_branch):
        up = add(lax.ppermute(up, "branch", turn(n_branch, 1)), resp_out[s]).astype(BF16)
    up = lax.ppermute(up, "branch", turn(n_branch, 1))
    resp_sum = (add(down, up) + resp_out[0].astype(F32)).astype(BF16)

    bit = 1
    while bit < n_branch:
        low = total.astype(BF16)
        total = add(low, lax.ppermute(low, "branch", [(i, i ^ bit) for i in range(n_branch)]))
        bit *= 2
    prompt_sum = total.astype(BF16)
    return (
        query_grad,
        resp_sum[:, :KV],
        resp_sum[:, KV:],
        prompt_sum[:, :KV],
        prompt_sum[:, KV:],
    )


def solution(mesh):
    in_specs = (
        P(("dp", "seq", "branch"), None),
        P(("dp", "seq", "branch"), None),
        P(("dp", "seq", "branch"), None),
        P(("dp", "seq", "branch"), None),
        P(("dp", "seq"), None),
        P(("dp", "seq"), None),
        P(("dp", "seq")),
    )
    out_specs = (
        P(("dp", "seq", "branch"), None),
        P(("dp", "seq", "branch"), None),
        P(("dp", "seq", "branch"), None),
        P(("dp", "seq"), None),
        P(("dp", "seq"), None),
    )
    return jax.shard_map(
        functools.partial(on_device, n_branch=mesh.shape["branch"]),
        mesh=mesh,
        in_specs=in_specs,
        out_specs=out_specs,
        check_vma=False,
    )
```

```python
import functools
import math

import jax
import jax.numpy as jnp
from jax import lax
from jax.experimental import pallas as pl
from jax.experimental.pallas import tpu as pltpu
from jax.sharding import PartitionSpec as P

HD = 128
HQ = 8
G = 2
KV = G * HD
SCALE = 1.0 / math.sqrt(HD)
LOG2_SCALE = SCALE * math.log2(math.e)
MASKED = -1e30
CHUNK = 512
SUB = 64
NEAR = (1, 2, 6, 7)
FAR = (3, 4, 5)
SENT = (1, 3, 5, 7, 4)
F32 = jnp.float32
BF16 = jnp.bfloat16


def fold(x, op):
    return op(x.reshape(x.shape[0] // 8, 8, x.shape[1]), axis=0)


def keys_of(kv, at, size, g):
    return kv[pl.ds(at, size), g * HD : (g + 1) * HD]


def values_of(kv, at, size, g):
    return kv[pl.ds(at, size), KV + g * HD : KV + (g + 1) * HD]


def causal(rows):
    key_pos = lax.broadcasted_iota(jnp.int32, (rows, rows), 0)
    row_pos = lax.broadcasted_iota(jnp.int32, (rows, rows), 1)
    return jnp.concatenate([key_pos <= row_pos] * HQ, axis=1)


def take_in(q_t, g_t, top, sums, kv, at, size, seen):
    step = size // len(seen)
    for g in range(G):
        s = jnp.dot(keys_of(kv, at, size, g), q_t[g], preferred_element_type=F32)
        dp = jnp.dot(values_of(kv, at, size, g), g_t[g], preferred_element_type=F32)
        parts = [slice(j * step, (j + 1) * step) for j in range(len(seen))]
        high = jnp.full((8, s.shape[1]), MASKED, F32)
        for ok, part in zip(seen, parts):
            high = jnp.maximum(high, jnp.where(ok, fold(s[part], jnp.max), MASKED))
        old = top[g]
        new = jnp.maximum(old, jnp.max(high, axis=0, keepdims=True) * LOG2_SCALE)
        keep = jnp.exp2(old - new)
        total, dots = sums[2 * g] * keep, sums[2 * g + 1] * keep
        for ok, part in zip(seen, parts):
            e = jnp.exp2(s[part] * LOG2_SCALE - (new + jnp.where(ok, 0.0, -MASKED)))
            total += fold(e, jnp.sum)
            dots += fold(e * dp[part], jnp.sum)
        top[g] = new
        sums[2 * g] = total
        sums[2 * g + 1] = dots


def give_back(q_t, g_t, lse, delta, dq, kv, at, size, seen, dst, to):
    step = size // len(seen)
    rows_rows = (((1,), (1,)), ((), ()))
    for g in range(G):
        keys = keys_of(kv, at, size, g)
        s = jnp.dot(keys, q_t[g], preferred_element_type=F32)
        dp = jnp.dot(values_of(kv, at, size, g), g_t[g], preferred_element_type=F32)
        p = []
        for j, ok in enumerate(seen):
            part = s[j * step : (j + 1) * step]
            if ok is None:
                part = jnp.where(causal(size), part * LOG2_SCALE - lse[g], MASKED)
            else:
                part = part * LOG2_SCALE - (lse[g] + jnp.where(ok, 0.0, -MASKED))
            p.append(jnp.exp2(part))
        p = jnp.concatenate(p, axis=0)
        ds = (p * (dp - delta[g])).astype(BF16)
        dk = lax.dot_general(ds, q_t[g], rows_rows, preferred_element_type=F32) * SCALE
        dv = lax.dot_general(p.astype(BF16), g_t[g], rows_rows, preferred_element_type=F32)
        dst[pl.ds(to, size), g * HD : (g + 1) * HD] = dk.astype(BF16)
        dst[pl.ds(to, size), KV + g * HD : KV + (g + 1) * HD] = dv.astype(BF16)
        dq[g] += jnp.dot(keys.T, ds, preferred_element_type=F32)


def prompt_chunks(blocks):
    return (blocks * SUB + CHUNK - 1) // CHUNK


def prompt_seen(blocks, t):
    return [t * (CHUNK // SUB) + j < blocks for j in range(CHUNK // SUB)]


def near_kernel(rows):
    def body(place, query, grad, own, prompt, *refs):
        near, (q_t, g_t, top, sums, kv) = refs[: len(NEAR)], refs[len(NEAR) :]
        blocks, branch = place[0], place[1]
        for g in range(G):
            for h in range(HQ):
                col = (g * HQ + h) * HD
                q_t[g, :, h * rows : (h + 1) * rows] = query[:, col : col + HD].T
                g_t[g, :, h * rows : (h + 1) * rows] = grad[:, col : col + HD].T
        seen = causal(rows)
        for g in range(G):
            s = jnp.dot(keys_of(own, 0, rows, g), q_t[g], preferred_element_type=F32)
            s = jnp.where(seen, s * LOG2_SCALE, MASKED)
            high = jnp.max(fold(s, jnp.max), axis=0, keepdims=True)
            dp = jnp.dot(values_of(own, 0, rows, g), g_t[g], preferred_element_type=F32)
            e = jnp.exp2(s - high)
            top[g] = high
            sums[2 * g] = fold(e, jnp.sum)
            sums[2 * g + 1] = fold(e * dp, jnp.sum)

        @pl.loop(0, prompt_chunks(blocks))
        def _(t):
            at = pl.multiple_of(t * CHUNK, CHUNK)
            take_in(q_t, g_t, top, sums, prompt, at, CHUNK, prompt_seen(blocks, t))

        for i, block in enumerate(near):
            kv[i * rows : (i + 1) * rows, :] = block[...]
        for i in range(0, len(NEAR), 2):

            @pl.when(branch >= NEAR[i])
            def _():
                take_in(q_t, g_t, top, sums, kv, i * rows, 2 * rows, [branch >= d for d in NEAR[i : i + 2]])

    return body


def prompt_kernel(rows, prompt_len):
    def body(place, q_t, g_t, top_in, sum_in, prompt, *refs):
        far = refs[: len(FAR)]
        lse, delta, dq, prompt_grad, top, sums = refs[len(FAR) :]
        blocks, branch = place[0], place[1]
        top[...] = top_in[...]
        sums[...] = sum_in[...]
        for block, distance in zip(far, FAR):

            @pl.when(branch >= distance)
            def _():
                take_in(q_t, g_t, top, sums, block, 0, rows, [True])

        for g in range(G):
            total = jnp.sum(sums[2 * g], axis=0, keepdims=True)
            lse[g] = top[g] + jnp.log2(total)
            delta[g] = jnp.sum(sums[2 * g + 1], axis=0, keepdims=True) / total
        dq[...] = jnp.zeros_like(dq)
        wide = prompt_chunks(blocks)
        for i in range(prompt_len // CHUNK):

            @pl.when(i >= wide)
            def _():
                prompt_grad[i * CHUNK : (i + 1) * CHUNK, :] = jnp.zeros((CHUNK, 2 * KV), BF16)

        @pl.loop(0, wide)
        def _(t):
            at = pl.multiple_of(t * CHUNK, CHUNK)
            give_back(q_t, g_t, lse, delta, dq, prompt, at, CHUNK, prompt_seen(blocks, t), prompt_grad, at)

    return body


def sent_kernel(rows):
    def body(place, q_t, g_t, lse, delta, dq_in, *refs):
        blocks, (down, up, last, dq, kv) = refs[: len(SENT)], refs[len(SENT) :]
        branch = place[1]
        dq[...] = dq_in[...]
        for i, block in enumerate(blocks):
            kv[i * rows : (i + 1) * rows, :] = block[...]
        for i, (distances, out) in enumerate(((SENT[:2], down), (SENT[2:4], up), (SENT[4:], last))):
            size = rows * len(distances)

            @pl.when(branch >= distances[0])
            def _():
                seen = [branch >= d for d in distances]
                give_back(q_t, g_t, lse, delta, dq, kv, 2 * i * rows, size, seen, out, 0)

            @pl.when(branch < distances[0])
            def _():
                out[...] = jnp.zeros((size, 2 * KV), BF16)

    return body


def kept_kernel(rows):
    def body(place, q_t, g_t, lse, delta, dq_in, own, block2, block6, out0, out2, out6, dq_out, dq):
        branch = place[1]
        dq[...] = dq_in[...]
        give_back(q_t, g_t, lse, delta, dq, own, 0, rows, [None], out0, 0)
        for distance, block, out in ((2, block2, out2), (6, block6, out6)):

            @pl.when(branch >= distance)
            def _():
                give_back(q_t, g_t, lse, delta, dq, block, 0, rows, [True], out, 0)

            @pl.when(branch < distance)
            def _():
                out[...] = jnp.zeros((rows, 2 * KV), BF16)

        for g in range(G):
            for h in range(HQ):
                col = (g * HQ + h) * HD
                dq_out[:, col : col + HD] = (dq[g, :, h * rows : (h + 1) * rows] * SCALE).T.astype(BF16)

    return body


def call(body, operands, out_shapes, scratch=(), flops=0, exps=0, fetched=(), put_back=()):
    count, outs = len(operands), len(out_shapes)

    def whole(*refs):
        sems = refs[-1]
        refs = list(refs[:-1])
        buffers = refs[count + outs + len(scratch) :]
        moved = [refs[i] for i in fetched] + [refs[count + i] for i in put_back]
        into = [pltpu.make_async_copy(moved[k], buffers[k], sems.at[k]) for k in range(len(fetched))]
        for copy in into:
            copy.start()
        for k, i in enumerate([*fetched, *(count + i for i in put_back)]):
            refs[i] = buffers[k]
        for copy in into:
            copy.wait()
        body(*refs[: count + outs + len(scratch)])
        back = [
            pltpu.make_async_copy(buffers[k], moved[k], sems.at[k]) for k in range(len(fetched), len(moved))
        ]
        for copy in back:
            copy.start()
        for copy in back:
            copy.wait()

    def space(i, x):
        return pltpu.HBM if i in fetched else pltpu.SMEM if x.ndim == 1 else pltpu.VMEM

    buffers = [pltpu.VMEM(operands[i].shape, operands[i].dtype) for i in fetched]
    buffers += [pltpu.VMEM(*out_shapes[i]) for i in put_back]
    return pl.pallas_call(
        whole,
        out_shape=[
            pltpu.HBM(*shape) if i in put_back else jax.ShapeDtypeStruct(*shape)
            for i, shape in enumerate(out_shapes)
        ],
        in_specs=[pl.BlockSpec(memory_space=space(i, x)) for i, x in enumerate(operands)],
        out_specs=[
            pl.BlockSpec(memory_space=pltpu.HBM if i in put_back else pltpu.VMEM) for i in range(outs)
        ],
        scratch_shapes=[
            *(pltpu.VMEM(shape, dtype) for shape, dtype in scratch),
            *buffers,
            pltpu.SemaphoreType.DMA((max(len(buffers), 1),)),
        ],
        compiler_params=pltpu.CompilerParams(vmem_limit_bytes=32 * 1024 * 1024),
        cost_estimate=pl.CostEstimate(flops=flops, bytes_accessed=1 << 20, transcendentals=exps),
    )(*(pltpu.with_memory_space_constraint(x, pltpu.HBM) if i in fetched else x for i, x in enumerate(operands)))


def pack(resp_key, resp_value, prompt_key, prompt_value, copies):
    def body(rk, rv, pk, pv, own, prompt):
        own[:, :KV] = rk[...]
        own[:, KV:] = rv[...]
        for i in range(copies):
            prompt[i, :, :KV] = pk[...]
            prompt[i, :, KV:] = pv[...]

    return pl.pallas_call(
        body,
        out_shape=[
            jax.ShapeDtypeStruct((resp_key.shape[0], 2 * KV), BF16),
            jax.ShapeDtypeStruct((copies, prompt_key.shape[0], 2 * KV), BF16),
        ],
    )(resp_key, resp_value, prompt_key, prompt_value)


def turn(n, step):
    return [(i, (i + step) % n) for i in range(n)]


def total_of(*terms):
    total = terms[0].astype(F32)
    for term in terms[1:]:
        total = total + term.astype(F32)
    return total


def on_device(query, resp_key, resp_value, out_grad, prompt_key, prompt_value, prefix_blocks, *, n_seq, n_branch):
    rows, shard = query.shape[0], prompt_key.shape[0]
    prompt_len, width = shard * n_seq, HQ * query.shape[0]

    def shift(x, step):
        return lax.ppermute(x, "branch", turn(n_branch, step))

    own, own_prompt = pack(resp_key, resp_value, prompt_key, prompt_value, n_seq)
    prompt = lax.all_to_all(own_prompt, "seq", 0, 0).reshape(prompt_len, 2 * KV)
    resp = {0: own, 1: shift(own, 1), 7: shift(own, -1), 2: shift(own, 2), 6: shift(own, -2)}
    resp[3], resp[4], resp[5] = shift(resp[2], 1), shift(resp[2], 2), shift(resp[6], -1)
    place = jnp.stack([prefix_blocks[0], lax.axis_index("branch")]).astype(jnp.int32)

    mac = 2 * G * width * HD
    top = ((G, 1, width), F32)
    sums = ((2 * G, 8, width), F32)
    turned = ((G, HD, width), BF16)
    dq_state = ((G, HD, width), F32)
    block = ((rows, 2 * KV), BF16)
    q_t, g_t, top0, sum0 = call(
        near_kernel(rows),
        [place, query, out_grad, own, prompt, *(resp[s] for s in NEAR)],
        [turned, turned, top, sums],
        [((rows * len(NEAR), 2 * KV), BF16)],
        flops=2 * mac * (prompt_len + 5 * rows),
    )
    lse, delta, dq, prompt_grad = call(
        prompt_kernel(rows, prompt_len),
        [place, q_t, g_t, top0, sum0, prompt, *(resp[s] for s in FAR)],
        [top, top, dq_state, ((prompt_len, 2 * KV), BF16)],
        [top, sums],
        flops=mac * (5 * prompt_len + 6 * rows),
        put_back=(2,),
    )
    pieces = lax.all_to_all(prompt_grad.reshape(n_seq, shard, 2 * KV), "seq", 0, 0)
    down, up, far, dq = call(
        sent_kernel(rows),
        [place, q_t, g_t, lse, delta, dq, *(resp[s] for s in SENT)],
        [((2 * rows, 2 * KV), BF16), ((2 * rows, 2 * KV), BF16), block, dq_state],
        [((rows * len(SENT), 2 * KV), BF16)],
        flops=5 * mac * rows * 5,
        fetched=(1, 2, 5),
    )
    grad0, grad2, grad6, query_grad = call(
        kept_kernel(rows),
        [place, q_t, g_t, lse, delta, dq, resp[0], resp[2], resp[6]],
        [block, block, block, (query.shape, BF16)],
        [dq_state],
        flops=5 * mac * rows * 3,
    )

    down, up, far = shift(down, -1), shift(up, 1), shift(far, -2)
    low = jnp.sum(pieces.astype(F32), axis=0).astype(BF16)
    low, grad2, grad6 = lax.optimization_barrier((low, grad2, grad6))
    flips = [low] + [
        lax.ppermute(low, "branch", [(i, i ^ k) for i in range(n_branch)]) for k in (1, 2, 3)
    ]
    from2 = shift(total_of(grad2, down[rows:], far).astype(BF16), -2)
    from6 = shift(total_of(grad6, up[:rows]).astype(BF16), 2)
    low = (total_of(flips[0], flips[1]) + total_of(flips[2], flips[3])).astype(BF16)
    prompt_sum = total_of(low, lax.ppermute(low, "branch", [(i, i ^ 4) for i in range(n_branch)])).astype(BF16)
    resp_sum = total_of(grad0, down[:rows], up[rows:], from2, from6).astype(BF16)
    return (
        query_grad,
        resp_sum[:, :KV],
        resp_sum[:, KV:],
        prompt_sum[:, :KV],
        prompt_sum[:, KV:],
    )


def solution(mesh):
    in_specs = (
        P(("dp", "seq", "branch"), None),
        P(("dp", "seq", "branch"), None),
        P(("dp", "seq", "branch"), None),
        P(("dp", "seq", "branch"), None),
        P(("dp", "seq"), None),
        P(("dp", "seq"), None),
        P(("dp", "seq")),
    )
    out_specs = (
        P(("dp", "seq", "branch"), None),
        P(("dp", "seq", "branch"), None),
        P(("dp", "seq", "branch"), None),
        P(("dp", "seq"), None),
        P(("dp", "seq"), None),
    )
    return jax.shard_map(
        functools.partial(on_device, n_seq=mesh.shape["seq"], n_branch=mesh.shape["branch"]),
        mesh=mesh,
        in_specs=in_specs,
        out_specs=out_specs,
        check_vma=False,
    )
```

```python
import functools
import math

import jax
import jax.numpy as jnp
from jax import lax
from jax.experimental import pallas as pl
from jax.experimental.pallas import tpu as pltpu
from jax.sharding import PartitionSpec as P

HD = 128
HQ = 8
G = 2
KV = G * HD
SCALE = 1.0 / math.sqrt(HD)
LOG2_SCALE = SCALE * math.log2(math.e)
MASKED = -1e30
CHUNK = 512
TILE = 256
PIECE = 128
SUB = 64
NEAR = (1, 2, 6, 7)
FAR = (3, 4, 5)
SENT = (1, 3, 5, 7, 4)
F32 = jnp.float32
BF16 = jnp.bfloat16


def fold(x, op):
    return op(x.reshape(x.shape[0] // 8, 8, x.shape[1]), axis=0)


def keys_of(kv, at, size, g):
    return kv[pl.ds(at, size), g * HD : (g + 1) * HD]


def values_of(kv, at, size, g):
    return kv[pl.ds(at, size), KV + g * HD : KV + (g + 1) * HD]


def causal(rows, width):
    key_pos = lax.broadcasted_iota(jnp.int32, (rows, rows), 0)
    row_pos = lax.broadcasted_iota(jnp.int32, (rows, rows), 1)
    return jnp.concatenate([key_pos <= row_pos] * (width // rows), axis=1)


def pieces_of(size, seen):
    piece = min(PIECE, size)
    if len(seen) * piece < size:
        seen = [ok for ok in seen for _ in range(size // piece // len(seen))]
    each = len(seen) * piece // size
    return [(k, piece, seen[k * len(seen) // size :][:each]) for k in range(0, size, piece)]


def over_parts(x, oks, step):
    x = x.reshape(x.shape[0] // 8, 8, x.shape[1])
    each = x.shape[0] // len(oks)
    return jnp.concatenate([step(x[i * each : (i + 1) * each], ok) for i, ok in enumerate(oks)], axis=0)


def take_in(q_t, g_t, top, sums, kv, at, size, seen):
    for g in range(G):
        for c in range(0, q_t.shape[2], TILE):
            cols = pl.ds(c, TILE)
            high, total, dots = top[g, :, cols], sums[2 * g, :, cols], sums[2 * g + 1, :, cols]
            for k, piece, oks in pieces_of(size, seen):
                s = jnp.dot(keys_of(kv, at + k, piece, g), q_t[g, :, cols], preferred_element_type=F32) * LOG2_SCALE
                dp = jnp.dot(values_of(kv, at + k, piece, g), g_t[g, :, cols], preferred_element_type=F32)
                each = piece // len(oks)
                new = high
                for i, ok in enumerate(oks):
                    new = jnp.maximum(new, jnp.where(ok, fold(s[i * each : (i + 1) * each], jnp.max), MASKED))
                keep = jnp.exp2(high - new)
                e = jnp.exp2(over_parts(s, oks, lambda x, ok: x - (new + jnp.where(ok, 0.0, -2 * MASKED))))
                total = total * keep + jnp.sum(e, axis=0)
                dots = dots * keep + jnp.sum(e * dp.reshape(piece // 8, 8, TILE), axis=0)
                high = new
            top[g, :, cols] = high
            sums[2 * g, :, cols] = total
            sums[2 * g + 1, :, cols] = dots


def give_back(q_t, g_t, lse, delta, dq, kv, at, size, seen, dst, to, p_buf, ds_buf):
    rows_rows = (((1,), (1,)), ((), ()))
    for g in range(G):
        for c in range(0, q_t.shape[2], TILE):
            cols = pl.ds(c, TILE)
            own = lse[g, :, cols]
            for k, piece, oks in pieces_of(size, seen):
                s = jnp.dot(keys_of(kv, at + k, piece, g), q_t[g, :, cols], preferred_element_type=F32) * LOG2_SCALE
                dp = jnp.dot(values_of(kv, at + k, piece, g), g_t[g, :, cols], preferred_element_type=F32)
                if oks[0] is None:
                    s = jnp.where(causal(size, TILE)[k : k + piece], s - own, MASKED)
                else:
                    s = over_parts(s, oks, lambda x, ok: x - (own + jnp.where(ok, 0.0, -2 * MASKED))).reshape(piece, TILE)
                p = jnp.exp2(s)
                p_buf[g, k : k + piece, cols] = p.astype(BF16)
                ds_buf[g, k : k + piece, cols] = (p * (dp - delta[g, :, cols])).astype(BF16)
        ds = ds_buf[g, :size, :]
        dk = lax.dot_general(ds, q_t[g], rows_rows, preferred_element_type=F32) * SCALE
        dv = lax.dot_general(p_buf[g, :size, :], g_t[g], rows_rows, preferred_element_type=F32)
        dst[pl.ds(to, size), g * HD : (g + 1) * HD] = dk.astype(BF16)
        dst[pl.ds(to, size), KV + g * HD : KV + (g + 1) * HD] = dv.astype(BF16)
        dq[g] += jnp.dot(keys_of(kv, at, size, g).T, ds, preferred_element_type=F32)


def prompt_chunks(blocks):
    return (blocks * SUB + CHUNK - 1) // CHUNK


def prompt_seen(blocks, t):
    return [t * (CHUNK // SUB) + j < blocks for j in range(CHUNK // SUB)]


def near_kernel(rows):
    def body(place, query, grad, own, prompt, *refs):
        near, (q_t, g_t, top, sums, kv) = refs[: len(NEAR)], refs[len(NEAR) :]
        blocks, branch = place[0], place[1]
        for g in range(G):
            for h in range(HQ):
                col = (g * HQ + h) * HD
                q_t[g, :, h * rows : (h + 1) * rows] = query[:, col : col + HD].T
                g_t[g, :, h * rows : (h + 1) * rows] = grad[:, col : col + HD].T
        seen = causal(rows, HQ * rows)
        for g in range(G):
            s = jnp.dot(keys_of(own, 0, rows, g), q_t[g], preferred_element_type=F32)
            s = jnp.where(seen, s * LOG2_SCALE, MASKED)
            high = fold(s, jnp.max)
            dp = jnp.dot(values_of(own, 0, rows, g), g_t[g], preferred_element_type=F32)
            e = jnp.exp2(s.reshape(rows // 8, 8, HQ * rows) - high).reshape(rows, HQ * rows)
            top[g] = high
            sums[2 * g] = fold(e, jnp.sum)
            sums[2 * g + 1] = fold(e * dp, jnp.sum)

        @pl.loop(0, prompt_chunks(blocks))
        def _(t):
            at = pl.multiple_of(t * CHUNK, CHUNK)
            take_in(q_t, g_t, top, sums, prompt, at, CHUNK, prompt_seen(blocks, t))

        for i, block in enumerate(near):
            kv[i * rows : (i + 1) * rows, :] = block[...]
        for i in range(0, len(NEAR), 2):

            @pl.when(branch >= NEAR[i])
            def _():
                take_in(q_t, g_t, top, sums, kv, i * rows, 2 * rows, [branch >= d for d in NEAR[i : i + 2]])

    return body


def prompt_kernel(rows, prompt_len):
    def body(place, q_t, g_t, top_in, sum_in, prompt, *refs):
        far = refs[: len(FAR)]
        lse, delta, dq, prompt_grad, top, sums, *bufs = refs[len(FAR) :]
        blocks, branch = place[0], place[1]
        top[...] = top_in[...]
        sums[...] = sum_in[...]
        for block, distance in zip(far, FAR):

            @pl.when(branch >= distance)
            def _():
                take_in(q_t, g_t, top, sums, block, 0, rows, [True])

        for g in range(G):
            high = jnp.max(top[g], axis=0, keepdims=True)
            keep = jnp.exp2(top[g] - high)
            total = jnp.sum(sums[2 * g] * keep, axis=0, keepdims=True)
            lse[g] = high + jnp.log2(total)
            delta[g] = jnp.sum(sums[2 * g + 1] * keep, axis=0, keepdims=True) / total
        dq[...] = jnp.zeros_like(dq)
        wide = prompt_chunks(blocks)
        for i in range(prompt_len // CHUNK):

            @pl.when(i >= wide)
            def _():
                prompt_grad[i * CHUNK : (i + 1) * CHUNK, :] = jnp.zeros((CHUNK, 2 * KV), BF16)

        @pl.loop(0, wide)
        def _(t):
            at = pl.multiple_of(t * CHUNK, CHUNK)
            give_back(q_t, g_t, lse, delta, dq, prompt, at, CHUNK, prompt_seen(blocks, t), prompt_grad, at, *bufs)

    return body


def sent_kernel(rows):
    def body(place, q_t, g_t, lse, delta, dq_in, *refs):
        blocks, (down, up, last, dq, kv, *bufs) = refs[: len(SENT)], refs[len(SENT) :]
        branch = place[1]
        dq[...] = dq_in[...]
        for i, block in enumerate(blocks):
            kv[i * rows : (i + 1) * rows, :] = block[...]
        for i, (distances, out) in enumerate(((SENT[:2], down), (SENT[2:4], up), (SENT[4:], last))):
            size = rows * len(distances)

            @pl.when(branch >= distances[0])
            def _():
                seen = [branch >= d for d in distances]
                give_back(q_t, g_t, lse, delta, dq, kv, 2 * i * rows, size, seen, out, 0, *bufs)

            @pl.when(branch < distances[0])
            def _():
                out[...] = jnp.zeros((size, 2 * KV), BF16)

    return body


def kept_kernel(rows):
    def body(place, q_t, g_t, lse, delta, dq_in, own, block2, block6, out0, out2, out6, dq_out, dq, *bufs):
        branch = place[1]
        dq[...] = dq_in[...]
        give_back(q_t, g_t, lse, delta, dq, own, 0, rows, [None], out0, 0, *bufs)
        for distance, block, out in ((2, block2, out2), (6, block6, out6)):

            @pl.when(branch >= distance)
            def _():
                give_back(q_t, g_t, lse, delta, dq, block, 0, rows, [True], out, 0, *bufs)

            @pl.when(branch < distance)
            def _():
                out[...] = jnp.zeros((rows, 2 * KV), BF16)

        for g in range(G):
            for h in range(HQ):
                col = (g * HQ + h) * HD
                dq_out[:, col : col + HD] = (dq[g, :, h * rows : (h + 1) * rows] * SCALE).T.astype(BF16)

    return body


def call(body, operands, out_shapes, scratch=(), flops=0, exps=0, fetched=(), put_back=()):
    count, outs = len(operands), len(out_shapes)

    def whole(*refs):
        sems = refs[-1]
        refs = list(refs[:-1])
        buffers = refs[count + outs + len(scratch) :]
        moved = [refs[i] for i in fetched] + [refs[count + i] for i in put_back]
        into = [pltpu.make_async_copy(moved[k], buffers[k], sems.at[k]) for k in range(len(fetched))]
        for copy in into:
            copy.start()
        for k, i in enumerate([*fetched, *(count + i for i in put_back)]):
            refs[i] = buffers[k]
        for copy in into:
            copy.wait()
        body(*refs[: count + outs + len(scratch)])
        back = [
            pltpu.make_async_copy(buffers[k], moved[k], sems.at[k]) for k in range(len(fetched), len(moved))
        ]
        for copy in back:
            copy.start()
        for copy in back:
            copy.wait()

    def space(i, x):
        return pltpu.HBM if i in fetched else pltpu.SMEM if x.ndim == 1 else pltpu.VMEM

    buffers = [pltpu.VMEM(operands[i].shape, operands[i].dtype) for i in fetched]
    buffers += [pltpu.VMEM(*out_shapes[i]) for i in put_back]
    return pl.pallas_call(
        whole,
        out_shape=[
            pltpu.HBM(*shape) if i in put_back else jax.ShapeDtypeStruct(*shape)
            for i, shape in enumerate(out_shapes)
        ],
        in_specs=[pl.BlockSpec(memory_space=space(i, x)) for i, x in enumerate(operands)],
        out_specs=[
            pl.BlockSpec(memory_space=pltpu.HBM if i in put_back else pltpu.VMEM) for i in range(outs)
        ],
        scratch_shapes=[
            *(pltpu.VMEM(shape, dtype) for shape, dtype in scratch),
            *buffers,
            pltpu.SemaphoreType.DMA((max(len(buffers), 1),)),
        ],
        compiler_params=pltpu.CompilerParams(vmem_limit_bytes=32 * 1024 * 1024),
        cost_estimate=pl.CostEstimate(flops=flops, bytes_accessed=1 << 20, transcendentals=exps),
    )(*(pltpu.with_memory_space_constraint(x, pltpu.HBM) if i in fetched else x for i, x in enumerate(operands)))


def pack(resp_key, resp_value, prompt_key, prompt_value, copies):
    def body(rk, rv, pk, pv, own, prompt):
        own[:, :KV] = rk[...]
        own[:, KV:] = rv[...]
        for i in range(copies):
            prompt[i, :, :KV] = pk[...]
            prompt[i, :, KV:] = pv[...]

    return pl.pallas_call(
        body,
        out_shape=[
            jax.ShapeDtypeStruct((resp_key.shape[0], 2 * KV), BF16),
            jax.ShapeDtypeStruct((copies, prompt_key.shape[0], 2 * KV), BF16),
        ],
    )(resp_key, resp_value, prompt_key, prompt_value)


def turn(n, step):
    return [(i, (i + step) % n) for i in range(n)]


def total_of(*terms):
    total = terms[0].astype(F32)
    for term in terms[1:]:
        total = total + term.astype(F32)
    return total


def on_device(query, resp_key, resp_value, out_grad, prompt_key, prompt_value, prefix_blocks, *, n_seq, n_branch):
    rows, shard = query.shape[0], prompt_key.shape[0]
    prompt_len, width = shard * n_seq, HQ * query.shape[0]

    def shift(x, step):
        return lax.ppermute(x, "branch", turn(n_branch, step))

    own, own_prompt = pack(resp_key, resp_value, prompt_key, prompt_value, n_seq)
    prompt = lax.all_to_all(own_prompt, "seq", 0, 0).reshape(prompt_len, 2 * KV)
    resp = {0: own, 1: shift(own, 1), 7: shift(own, -1), 2: shift(own, 2), 6: shift(own, -2)}
    resp[3], resp[4], resp[5] = shift(resp[2], 1), shift(resp[2], 2), shift(resp[6], -1)
    place = jnp.stack([prefix_blocks[0], lax.axis_index("branch")]).astype(jnp.int32)

    mac = 2 * G * width * HD
    row = ((G, 1, width), F32)
    top = ((G, 8, width), F32)
    sums = ((2 * G, 8, width), F32)
    turned = ((G, HD, width), BF16)
    dq_state = ((G, HD, width), F32)
    block = ((rows, 2 * KV), BF16)

    def probs(keys):
        return ((G, keys, width), BF16)

    q_t, g_t, top0, sum0 = call(
        near_kernel(rows),
        [place, query, out_grad, own, prompt, *(resp[s] for s in NEAR)],
        [turned, turned, top, sums],
        [((rows * len(NEAR), 2 * KV), BF16)],
        flops=2 * mac * (prompt_len + 5 * rows),
    )
    lse, delta, dq, prompt_grad = call(
        prompt_kernel(rows, prompt_len),
        [place, q_t, g_t, top0, sum0, prompt, *(resp[s] for s in FAR)],
        [row, row, dq_state, ((prompt_len, 2 * KV), BF16)],
        [top, sums, probs(CHUNK), probs(CHUNK)],
        flops=mac * (5 * prompt_len + 6 * rows),
        put_back=(2,),
    )
    pieces = lax.all_to_all(prompt_grad.reshape(n_seq, shard, 2 * KV), "seq", 0, 0)
    down, up, far, dq = call(
        sent_kernel(rows),
        [place, q_t, g_t, lse, delta, dq, *(resp[s] for s in SENT)],
        [((2 * rows, 2 * KV), BF16), ((2 * rows, 2 * KV), BF16), block, dq_state],
        [((rows * len(SENT), 2 * KV), BF16), probs(2 * rows), probs(2 * rows)],
        flops=5 * mac * rows * 5,
        fetched=(1, 2, 5),
    )
    grad0, grad2, grad6, query_grad = call(
        kept_kernel(rows),
        [place, q_t, g_t, lse, delta, dq, resp[0], resp[2], resp[6]],
        [block, block, block, (query.shape, BF16)],
        [dq_state, probs(rows), probs(rows)],
        flops=5 * mac * rows * 3,
    )

    down, up, far = shift(down, -1), shift(up, 1), shift(far, -2)
    low = jnp.sum(pieces.astype(F32), axis=0).astype(BF16)
    low, grad2, grad6 = lax.optimization_barrier((low, grad2, grad6))
    flips = [low] + [
        lax.ppermute(low, "branch", [(i, i ^ k) for i in range(n_branch)]) for k in (1, 2, 3)
    ]
    from2 = shift(total_of(grad2, down[rows:], far).astype(BF16), -2)
    from6 = shift(total_of(grad6, up[:rows]).astype(BF16), 2)
    low = (total_of(flips[0], flips[1]) + total_of(flips[2], flips[3])).astype(BF16)
    prompt_sum = total_of(low, lax.ppermute(low, "branch", [(i, n_branch - 1 - i) for i in range(n_branch)])).astype(BF16)
    resp_sum = total_of(grad0, down[:rows], up[rows:], from2, from6).astype(BF16)
    return (
        query_grad,
        resp_sum[:, :KV],
        resp_sum[:, KV:],
        prompt_sum[:, :KV],
        prompt_sum[:, KV:],
    )


def solution(mesh):
    in_specs = (
        P(("dp", "seq", "branch"), None),
        P(("dp", "seq", "branch"), None),
        P(("dp", "seq", "branch"), None),
        P(("dp", "seq", "branch"), None),
        P(("dp", "seq"), None),
        P(("dp", "seq"), None),
        P(("dp", "seq")),
    )
    out_specs = (
        P(("dp", "seq", "branch"), None),
        P(("dp", "seq", "branch"), None),
        P(("dp", "seq", "branch"), None),
        P(("dp", "seq"), None),
        P(("dp", "seq"), None),
    )
    return jax.shard_map(
        functools.partial(on_device, n_seq=mesh.shape["seq"], n_branch=mesh.shape["branch"]),
        mesh=mesh,
        in_specs=in_specs,
        out_specs=out_specs,
        check_vma=False,
    )
```

```python
import functools
import math

import jax
import jax.numpy as jnp
from jax import lax
from jax.experimental import pallas as pl
from jax.experimental.pallas import tpu as pltpu
from jax.sharding import PartitionSpec as P

HD = 128
HQ = 8
G = 2
KV = G * HD
SCALE = 1.0 / math.sqrt(HD)
LOG2_SCALE = SCALE * math.log2(math.e)
MASKED = -1e30
CHUNK = 512
TILE = 256
PIECE = 128
SUB = 64
NEAR = (1, 2, 6, 7)
FAR = (3, 4, 5)
SENT = (1, 3, 5, 7, 4)
F32 = jnp.float32
BF16 = jnp.bfloat16


def fold(x, op):
    return op(x.reshape(x.shape[0] // 8, 8, x.shape[1]), axis=0)


def keys_of(kv, at, size, g):
    return kv[pl.ds(at, size), g * HD : (g + 1) * HD]


def values_of(kv, at, size, g):
    return kv[pl.ds(at, size), KV + g * HD : KV + (g + 1) * HD]


def causal(rows, width):
    key_pos = lax.broadcasted_iota(jnp.int32, (rows, rows), 0)
    row_pos = lax.broadcasted_iota(jnp.int32, (rows, rows), 1)
    return jnp.concatenate([key_pos <= row_pos] * (width // rows), axis=1)


def pieces_of(size, seen):
    piece = min(PIECE, size)
    if len(seen) * piece < size:
        seen = [ok for ok in seen for _ in range(size // piece // len(seen))]
    each = len(seen) * piece // size
    return [(k, piece, seen[k * len(seen) // size :][:each]) for k in range(0, size, piece)]


def over_parts(x, oks, step):
    x = x.reshape(x.shape[0] // 8, 8, x.shape[1])
    each = x.shape[0] // len(oks)
    return jnp.concatenate([step(x[i * each : (i + 1) * each], ok) for i, ok in enumerate(oks)], axis=0)


def take_in(q_t, g_t, top, sums, kv, at, size, seen):
    for g in range(G):
        for c in range(0, q_t.shape[2], TILE):
            cols = pl.ds(c, TILE)
            high, total, dots = top[g, :, cols], sums[2 * g, :, cols], sums[2 * g + 1, :, cols]
            for k, piece, oks in pieces_of(size, seen):
                s = jnp.dot(keys_of(kv, at + k, piece, g), q_t[g, :, cols], preferred_element_type=F32) * LOG2_SCALE
                dp = jnp.dot(values_of(kv, at + k, piece, g), g_t[g, :, cols], preferred_element_type=F32)
                each = piece // len(oks)
                new = high
                for i, ok in enumerate(oks):
                    new = jnp.maximum(new, jnp.where(ok, fold(s[i * each : (i + 1) * each], jnp.max), MASKED))
                keep = jnp.exp2(high - new)
                e = jnp.exp2(over_parts(s, oks, lambda x, ok: x - (new + jnp.where(ok, 0.0, -2 * MASKED))))
                total = total * keep + jnp.sum(e, axis=0)
                dots = dots * keep + jnp.sum(e * dp.reshape(piece // 8, 8, TILE), axis=0)
                high = new
            top[g, :, cols] = high
            sums[2 * g, :, cols] = total
            sums[2 * g + 1, :, cols] = dots


def give_back(q_t, g_t, lse, delta, dq, kv, at, size, seen, dst, to, p_buf, ds_buf):
    rows_rows = (((1,), (1,)), ((), ()))
    for g in range(G):
        for c in range(0, q_t.shape[2], TILE):
            cols = pl.ds(c, TILE)
            own = lse[g, :, cols]
            for k, piece, oks in pieces_of(size, seen):
                s = jnp.dot(keys_of(kv, at + k, piece, g), q_t[g, :, cols], preferred_element_type=F32) * LOG2_SCALE
                dp = jnp.dot(values_of(kv, at + k, piece, g), g_t[g, :, cols], preferred_element_type=F32)
                if oks[0] is None:
                    s = jnp.where(causal(size, TILE)[k : k + piece], s - own, MASKED)
                else:
                    s = over_parts(s, oks, lambda x, ok: x - (own + jnp.where(ok, 0.0, -2 * MASKED))).reshape(piece, TILE)
                p = jnp.exp2(s)
                p_buf[g, k : k + piece, cols] = p.astype(BF16)
                ds_buf[g, k : k + piece, cols] = (p * (dp - delta[g, :, cols])).astype(BF16)
        ds = ds_buf[g, :size, :]
        dk = lax.dot_general(ds, q_t[g], rows_rows, preferred_element_type=F32) * SCALE
        dv = lax.dot_general(p_buf[g, :size, :], g_t[g], rows_rows, preferred_element_type=F32)
        dst[pl.ds(to, size), g * HD : (g + 1) * HD] = dk.astype(BF16)
        dst[pl.ds(to, size), KV + g * HD : KV + (g + 1) * HD] = dv.astype(BF16)
        dq[g] += jnp.dot(keys_of(kv, at, size, g).T, ds, preferred_element_type=F32)


def prompt_chunks(blocks):
    return (blocks * SUB + CHUNK - 1) // CHUNK


def prompt_seen(blocks, t):
    return [t * (CHUNK // SUB) + j < blocks for j in range(CHUNK // SUB)]


def near_kernel(rows):
    def body(place, query, grad, own, prompt, *refs):
        near, (q_t, g_t, top, sums, kv) = refs[: len(NEAR)], refs[len(NEAR) :]
        blocks, branch = place[0], place[1]
        for g in range(G):
            for h in range(HQ):
                col = (g * HQ + h) * HD
                q_t[g, :, h * rows : (h + 1) * rows] = query[:, col : col + HD].T
                g_t[g, :, h * rows : (h + 1) * rows] = grad[:, col : col + HD].T
        seen = causal(rows, HQ * rows)
        for g in range(G):
            s = jnp.dot(keys_of(own, 0, rows, g), q_t[g], preferred_element_type=F32)
            s = jnp.where(seen, s * LOG2_SCALE, MASKED)
            high = fold(s, jnp.max)
            dp = jnp.dot(values_of(own, 0, rows, g), g_t[g], preferred_element_type=F32)
            e = jnp.exp2(s.reshape(rows // 8, 8, HQ * rows) - high).reshape(rows, HQ * rows)
            top[g] = high
            sums[2 * g] = fold(e, jnp.sum)
            sums[2 * g + 1] = fold(e * dp, jnp.sum)

        @pl.loop(0, prompt_chunks(blocks))
        def _(t):
            at = pl.multiple_of(t * CHUNK, CHUNK)
            take_in(q_t, g_t, top, sums, prompt, at, CHUNK, prompt_seen(blocks, t))

        for i, block in enumerate(near):
            kv[i * rows : (i + 1) * rows, :] = block[...]
        for i in range(0, len(NEAR), 2):

            @pl.when(branch >= NEAR[i])
            def _():
                take_in(q_t, g_t, top, sums, kv, i * rows, 2 * rows, [branch >= d for d in NEAR[i : i + 2]])

    return body


def prompt_kernel(rows, prompt_len):
    def body(place, q_t, g_t, top_in, sum_in, prompt, *refs):
        far = refs[: len(FAR)]
        lse, delta, dq_out, prompt_grad, top, sums, dq, *bufs = refs[len(FAR) :]
        blocks, branch = place[0], place[1]
        top[...] = top_in[...]
        sums[...] = sum_in[...]
        for block, distance in zip(far, FAR):

            @pl.when(branch >= distance)
            def _():
                take_in(q_t, g_t, top, sums, block, 0, rows, [True])

        for g in range(G):
            high = jnp.max(top[g], axis=0, keepdims=True)
            keep = jnp.exp2(top[g] - high)
            total = jnp.sum(sums[2 * g] * keep, axis=0, keepdims=True)
            lse[g] = high + jnp.log2(total)
            delta[g] = jnp.sum(sums[2 * g + 1] * keep, axis=0, keepdims=True) / total
        dq[...] = jnp.zeros_like(dq)
        wide = prompt_chunks(blocks)
        for i in range(prompt_len // CHUNK):

            @pl.when(i >= wide)
            def _():
                prompt_grad[i * CHUNK : (i + 1) * CHUNK, :] = jnp.zeros((CHUNK, 2 * KV), BF16)

        @pl.loop(0, wide)
        def _(t):
            at = pl.multiple_of(t * CHUNK, CHUNK)
            give_back(q_t, g_t, lse, delta, dq, prompt, at, CHUNK, prompt_seen(blocks, t), prompt_grad, at, *bufs)

        dq_out[...] = dq[...].astype(BF16)

    return body


def sent_kernel(rows):
    def body(place, q_t, g_t, lse, delta, dq_in, *refs):
        blocks, (down, up, last, dq, kv, *bufs) = refs[: len(SENT)], refs[len(SENT) :]
        branch = place[1]
        dq[...] = jnp.zeros_like(dq)
        for i, block in enumerate(blocks):
            kv[i * rows : (i + 1) * rows, :] = block[...]
        for i, (distances, out) in enumerate(((SENT[:2], down), (SENT[2:4], up), (SENT[4:], last))):
            size = rows * len(distances)

            @pl.when(branch >= distances[0])
            def _():
                seen = [branch >= d for d in distances]
                give_back(q_t, g_t, lse, delta, dq, kv, 2 * i * rows, size, seen, out, 0, *bufs)

            @pl.when(branch < distances[0])
            def _():
                out[...] = jnp.zeros((size, 2 * KV), BF16)

        dq[...] += dq_in().astype(F32)

    return body


def kept_kernel(rows):
    def body(place, q_t, g_t, lse, delta, dq_in, own, block2, block6, out0, out2, out6, dq_out, dq, *bufs):
        branch = place[1]
        dq[...] = dq_in[...]
        give_back(q_t, g_t, lse, delta, dq, own, 0, rows, [None], out0, 0, *bufs)
        for distance, block, out in ((2, block2, out2), (6, block6, out6)):

            @pl.when(branch >= distance)
            def _():
                give_back(q_t, g_t, lse, delta, dq, block, 0, rows, [True], out, 0, *bufs)

            @pl.when(branch < distance)
            def _():
                out[...] = jnp.zeros((rows, 2 * KV), BF16)

        for g in range(G):
            for h in range(HQ):
                col = (g * HQ + h) * HD
                dq_out[:, col : col + HD] = (dq[g, :, h * rows : (h + 1) * rows] * SCALE).T.astype(BF16)

    return body


def call(body, operands, out_shapes, scratch=(), flops=0, exps=0, fetched=(), put_back=()):
    count, outs = len(operands), len(out_shapes)

    def whole(*refs):
        sems = refs[-1]
        refs = list(refs[:-1])
        buffers = refs[count + outs + len(scratch) :]
        moved = [refs[i] for i in fetched] + [refs[count + i] for i in put_back]
        into = [pltpu.make_async_copy(moved[k], buffers[k], sems.at[k]) for k in range(len(fetched))]
        for copy in into:
            copy.start()
        for k, i in enumerate([*fetched, *(count + i for i in put_back)]):
            refs[i] = buffers[k]
        for copy in into[:-1]:
            copy.wait()
        if into:

            def arrived(buffer=refs[fetched[-1]]):
                into[-1].wait()
                return buffer[...]

            refs[fetched[-1]] = arrived
        body(*refs[: count + outs + len(scratch)])
        back = [
            pltpu.make_async_copy(buffers[k], moved[k], sems.at[k]) for k in range(len(fetched), len(moved))
        ]
        for copy in back:
            copy.start()
        for copy in back:
            copy.wait()

    def space(i, x):
        return pltpu.HBM if i in fetched else pltpu.SMEM if x.ndim == 1 else pltpu.VMEM

    buffers = [pltpu.VMEM(operands[i].shape, operands[i].dtype) for i in fetched]
    buffers += [pltpu.VMEM(*out_shapes[i]) for i in put_back]
    return pl.pallas_call(
        whole,
        out_shape=[
            pltpu.HBM(*shape) if i in put_back else jax.ShapeDtypeStruct(*shape)
            for i, shape in enumerate(out_shapes)
        ],
        in_specs=[pl.BlockSpec(memory_space=space(i, x)) for i, x in enumerate(operands)],
        out_specs=[
            pl.BlockSpec(memory_space=pltpu.HBM if i in put_back else pltpu.VMEM) for i in range(outs)
        ],
        scratch_shapes=[
            *(pltpu.VMEM(shape, dtype) for shape, dtype in scratch),
            *buffers,
            pltpu.SemaphoreType.DMA((max(len(buffers), 1),)),
        ],
        compiler_params=pltpu.CompilerParams(vmem_limit_bytes=32 * 1024 * 1024),
        cost_estimate=pl.CostEstimate(flops=flops, bytes_accessed=1 << 20, transcendentals=exps),
    )(*(pltpu.with_memory_space_constraint(x, pltpu.HBM) if i in fetched else x for i, x in enumerate(operands)))


def pack(resp_key, resp_value, prompt_key, prompt_value, copies):
    def body(rk, rv, pk, pv, own, prompt):
        own[:, :KV] = rk[...]
        own[:, KV:] = rv[...]
        for i in range(copies):
            prompt[i, :, :KV] = pk[...]
            prompt[i, :, KV:] = pv[...]

    return pl.pallas_call(
        body,
        out_shape=[
            jax.ShapeDtypeStruct((resp_key.shape[0], 2 * KV), BF16),
            jax.ShapeDtypeStruct((copies, prompt_key.shape[0], 2 * KV), BF16),
        ],
    )(resp_key, resp_value, prompt_key, prompt_value)


def turn(n, step):
    return [(i, (i + step) % n) for i in range(n)]


def total_of(*terms):
    total = terms[0].astype(F32)
    for term in terms[1:]:
        total = total + term.astype(F32)
    return total


def on_device(query, resp_key, resp_value, out_grad, prompt_key, prompt_value, prefix_blocks, *, n_seq, n_branch):
    rows, shard = query.shape[0], prompt_key.shape[0]
    prompt_len, width = shard * n_seq, HQ * query.shape[0]

    def shift(x, step):
        return lax.ppermute(x, "branch", turn(n_branch, step))

    own, own_prompt = pack(resp_key, resp_value, prompt_key, prompt_value, n_seq)
    prompt = lax.all_to_all(own_prompt, "seq", 0, 0).reshape(prompt_len, 2 * KV)
    resp = {0: own, 1: shift(own, 1), 7: shift(own, -1), 2: shift(own, 2), 6: shift(own, -2)}
    resp[3], resp[4], resp[5] = shift(resp[2], 1), shift(resp[2], 2), shift(resp[6], -1)
    place = jnp.stack([prefix_blocks[0], lax.axis_index("branch")]).astype(jnp.int32)

    mac = 2 * G * width * HD
    row = ((G, 1, width), F32)
    top = ((G, 8, width), F32)
    sums = ((2 * G, 8, width), F32)
    turned = ((G, HD, width), BF16)
    dq_state = ((G, HD, width), F32)
    block = ((rows, 2 * KV), BF16)

    def probs(keys):
        return ((G, keys, width), BF16)

    q_t, g_t, top0, sum0 = call(
        near_kernel(rows),
        [place, query, out_grad, own, prompt, *(resp[s] for s in NEAR)],
        [turned, turned, top, sums],
        [((rows * len(NEAR), 2 * KV), BF16)],
        flops=2 * mac * (prompt_len + 5 * rows),
    )
    lse, delta, dq, prompt_grad = call(
        prompt_kernel(rows, prompt_len),
        [place, q_t, g_t, top0, sum0, prompt, *(resp[s] for s in FAR)],
        [row, row, turned, ((prompt_len, 2 * KV), BF16)],
        [top, sums, dq_state, probs(CHUNK), probs(CHUNK)],
        flops=mac * (5 * prompt_len + 6 * rows),
        put_back=(2,),
    )
    pieces = lax.all_to_all(prompt_grad.reshape(n_seq, shard, 2 * KV), "seq", 0, 0)
    down, up, far, dq = call(
        sent_kernel(rows),
        [place, q_t, g_t, lse, delta, dq, *(resp[s] for s in SENT)],
        [((2 * rows, 2 * KV), BF16), ((2 * rows, 2 * KV), BF16), block, dq_state],
        [((rows * len(SENT), 2 * KV), BF16), probs(2 * rows), probs(2 * rows)],
        flops=5 * mac * rows * 5,
        fetched=(1, 2, 5),
    )
    grad0, grad2, grad6, query_grad = call(
        kept_kernel(rows),
        [place, q_t, g_t, lse, delta, dq, resp[0], resp[2], resp[6]],
        [block, block, block, (query.shape, BF16)],
        [dq_state, probs(rows), probs(rows)],
        flops=5 * mac * rows * 3,
    )

    down, up, far = shift(down, -1), shift(up, 1), shift(far, -2)
    low = jnp.sum(pieces.astype(F32), axis=0).astype(BF16)
    low, grad2, grad6 = lax.optimization_barrier((low, grad2, grad6))
    flips = [low] + [
        lax.ppermute(low, "branch", [(i, i ^ k) for i in range(n_branch)]) for k in (1, 2, 3)
    ]
    from2 = shift(total_of(grad2, down[rows:], far).astype(BF16), -2)
    from6 = shift(total_of(grad6, up[:rows]).astype(BF16), 2)
    low = (total_of(flips[0], flips[1]) + total_of(flips[2], flips[3])).astype(BF16)
    prompt_sum = total_of(low, lax.ppermute(low, "branch", [(i, n_branch - 1 - i) for i in range(n_branch)])).astype(BF16)
    resp_sum = total_of(grad0, down[:rows], up[rows:], from2, from6).astype(BF16)
    return (
        query_grad,
        resp_sum[:, :KV],
        resp_sum[:, KV:],
        prompt_sum[:, :KV],
        prompt_sum[:, KV:],
    )


def solution(mesh):
    in_specs = (
        P(("dp", "seq", "branch"), None),
        P(("dp", "seq", "branch"), None),
        P(("dp", "seq", "branch"), None),
        P(("dp", "seq", "branch"), None),
        P(("dp", "seq"), None),
        P(("dp", "seq"), None),
        P(("dp", "seq")),
    )
    out_specs = (
        P(("dp", "seq", "branch"), None),
        P(("dp", "seq", "branch"), None),
        P(("dp", "seq", "branch"), None),
        P(("dp", "seq"), None),
        P(("dp", "seq"), None),
    )
    return jax.shard_map(
        functools.partial(on_device, n_seq=mesh.shape["seq"], n_branch=mesh.shape["branch"]),
        mesh=mesh,
        in_specs=in_specs,
        out_specs=out_specs,
        check_vma=False,
    )
```
